32 devices in a mesh: basis: 4 (over x, core), fit: 8 (over z, y).
Axes of the slice: x: 2, y: 2, z: 4, core: 2. Of those that a mesh axis runs over, the one named last changes fastest.
Arguments:
- integrals: bfloat16 [512, 128, 1024], P('basis', 'fit'), may hold values from -6 to 6
- pair_mask: int32 [32, 64], replicated, may hold values 0 or 1
- row_blocks: int32 [32], replicated, may hold values from 0 to 31, each once
- occ_coef: bfloat16 [512, 64], P('basis'), may hold values from -0.375 to 0.375
- vir_coef: bfloat16 [1024, 8192], P(None, 'fit'), may hold values from -0.1875 to 0.1875
Outputs:
- transformed: bfloat16 [128, 64, 8192], P(None, 'basis', 'fit')
The draws below stay inside these ranges and needn't reach their ends.
Inputs may be any that keep to these rules, and one draw needn't show every extreme that they name: `row_blocks`: each of the 32 atom blocks appears exactly once. `pair_mask`: 1 marks a significant pair of atom blocks.
All inputs are finite; a program needn't handle non-finite values.
Results may differ from the reference program's by a relative error of at most 0.0049.
Values may be sent and summed in bfloat16 or wider, within the bound.
No kernel may reach another device: no remote copies, remote signals or barrier semaphores. Data moves between devices by JAX's collectives and lax.ppermute only.
A program may use at most 128 MiB of HBM per device.

```python
import jax
import jax.numpy as jnp
from jax import lax

BLK = 16
NU = 1024
FIT_DEV = 16
NOCC = 64
NMU = 512
NP = 128
NVIRW = 8192
NMB = 32
NNB = 64
N_FIT = 8


def with_ends(values, stream_key, least, top_value):
    place = [jax.random.randint(jax.random.fold_in(stream_key, axis), (), 0, length) for axis, length in enumerate(values.shape)]
    longest = values.shape.index(max(values.shape))
    beside = place[:longest] + [(place[longest] + 1) % values.shape[longest]] + place[longest + 1:]
    return values.at[tuple(place)].set(least).at[tuple(beside)].set(top_value)


def raised(values, own_key, source, target, blocks, factor):
    owner, partner = [(jnp.arange(values.shape[position]) // (values.shape[position] // blocks)).reshape([-1 if axis == position else 1 for axis in range(values.ndim)]) for position in (source, target)]
    chosen = jax.random.permutation(own_key, blocks)[partner]
    strong = (owner == chosen) | (owner == (partner + blocks // 2) % blocks)
    return jnp.where(strong, factor * values, values)


def shard_levels(rng, shape, cuts, low, high):
    def one(axis_at, shards_of):
        heights = jax.random.uniform(jax.random.fold_in(jax.random.fold_in(rng, 6), axis_at), (shards_of,), jnp.float32, low / len(cuts), high / len(cuts))
        return jnp.repeat(jnp.exp(heights), shape[axis_at] // shards_of).reshape((-1,) + (1,) * (len(shape) - axis_at - 1))

    loudness = one(*cuts[0])
    for cut in cuts[1:]:
        loudness = loudness * one(*cut)
    return loudness


def bell_draw(key, shape, spread, bound, shards=(), kind=jnp.bfloat16):
    values = spread * jax.random.normal(key, shape, jnp.float32)
    if shards:
        values = values * shard_levels(key, shape, shards, -0.22, 0.18)
    return jnp.clip(values, -bound, bound).astype(kind)


def heavy_noise(stream_key, shape, deviation, bound, split, heavy, kind=jnp.bfloat16):
    drawn = deviation * jax.random.normal(stream_key, shape, jnp.float32)
    if split:
        drawn = drawn * shard_levels(stream_key, shape, split, -0.22, 0.18)
    return jnp.clip(raised(drawn, jax.random.fold_in(stream_key, 3), *heavy), -bound, bound).astype(kind)


def setup_inputs(seed: int = 0) -> dict:
    streams_of = jax.random.split(jax.random.key(seed), 6)
    integrals = bell_draw(streams_of[0], (NMU, NP, NU), 1.0, 6.0, ((0, 4), (1, 8)))
    pair_mask = with_ends((jax.random.randint(streams_of[1], (NMB, NNB), 0, 3) < 2).astype(jnp.int32), jax.random.fold_in(streams_of[1], 1), 0, 1)
    row_blocks = jax.random.permutation(streams_of[2], NMB).astype(jnp.int32)
    occ_coef = heavy_noise(streams_of[3], (NMU, NOCC), NMU ** -0.5, 0.375, ((0, 4),), (0, 1, 4, 2.0))
    vir_coef = bell_draw(streams_of[4], (NU, NVIRW), NU ** -0.5, 0.1875, ((1, 8),))
    return dict(integrals=integrals, pair_mask=pair_mask, row_blocks=row_blocks, occ_coef=occ_coef, vir_coef=vir_coef)


def reference(integrals, pair_mask, row_blocks, occ_coef, vir_coef):
    blocks = occ_coef.reshape(NMB, BLK, NOCC)
    occ_rows = jnp.take(blocks, row_blocks.astype(jnp.int32), axis=0)
    mask_rows = jnp.take(pair_mask, row_blocks.astype(jnp.int32), axis=0)
    mask_full = jnp.repeat(mask_rows, BLK, axis=1).astype(jnp.bfloat16)
    x_blocks = integrals.reshape(NMB, BLK, NP, NU)

    def add_block(total, item):
        x_block, c_block, m_block = item
        masked = (x_block * m_block[None, None, :]).reshape(BLK, NP * NU)
        term = lax.dot_general(c_block, masked, (((0,), (0,)), ((), ())), preferred_element_type=jnp.float32)
        return total + term, None

    start = jnp.zeros((NOCC, NP * NU), jnp.float32)
    total, _ = lax.scan(add_block, start, (x_blocks, occ_rows, mask_full))
    half = total.astype(jnp.bfloat16).reshape(NOCC, NP, NU)
    half = jnp.transpose(half, (1, 0, 2)).reshape(N_FIT, FIT_DEV * NOCC, NU)

    def project(group):
        return jnp.dot(group, vir_coef, preferred_element_type=jnp.float32).astype(jnp.bfloat16)

    result = lax.map(project, half)
    return result.reshape(NP, NOCC, NVIRW)
```

```python
import functools

import jax
import jax.numpy as jnp
from jax import lax
from jax.experimental import pallas as pl
from jax.experimental.pallas import tpu as pltpu
from jax.sharding import PartitionSpec as P

BLK = 16
CHUNKS = 2
ZS, YS = 4, 2
TILE = 256

CORE_SWAP = [(0, 1), (1, 0), (2, 3), (3, 2)]
X_SWAP = [(0, 2), (2, 0), (1, 3), (3, 1)]
Y_SWAP = [(f, f ^ 1) for f in range(ZS * YS)]
Z_RING = [(f, (f + YS) % (ZS * YS)) for f in range(ZS * YS)]


def half_kernel(chunk, p_chunk, fit_dev, share, scal, occ_ref, pm_ref, x_ref, own_ref, send_ref, w_ref, m_ref):
    nblk = scal.shape[0] - 4
    step = pl.program_id(0)
    depth = BLK * fit_dev

    @pl.when(step == 0)
    def _():
        lane = lax.broadcasted_iota(jnp.int32, (BLK, depth), 1)
        row = lax.broadcasted_iota(jnp.int32, (BLK, depth), 0)
        spread = (lane // fit_dev == row).astype(jnp.float32).astype(jnp.bfloat16)
        pos = lax.broadcasted_iota(jnp.int32, (share, depth), 1) % fit_dev
        for b in range(nblk):
            rb = scal[4 + b]
            occ_b = occ_ref[pl.ds(pl.multiple_of(rb * BLK, BLK), BLK), :]
            wide = lax.dot_general(occ_b, spread, (((0,), (0,)), ((), ())), preferred_element_type=jnp.float32)
            m_ref[pl.ds(b, 1), :] = pm_ref[pl.ds(rb, 1), :].astype(jnp.float32)
            for d in range(4):
                part = wide[d * share : (d + 1) * share, :]
                for p in range(p_chunk):
                    val = jnp.where(pos == chunk * p_chunk + p, part, 0.0).astype(jnp.bfloat16)
                    base = scal[d] * (p_chunk * share) + p * share
                    w_ref[pl.ds(pl.multiple_of(base, share), share), b * depth : (b + 1) * depth] = val

    nnb = pm_ref.shape[1]
    tile = x_ref.shape[1]
    col = (lax.broadcasted_iota(jnp.int32, (nnb, tile), 1) + step * tile) // BLK
    blk = lax.broadcasted_iota(jnp.int32, (nnb, tile), 0)
    pick = (col == blk).astype(jnp.float32).astype(jnp.bfloat16)
    mask = jnp.dot(m_ref[...].astype(jnp.bfloat16), pick, preferred_element_type=jnp.float32).astype(jnp.bfloat16)
    xm = jnp.concatenate(
        [x_ref[b * depth : (b + 1) * depth, :] * mask[b : b + 1, :] for b in range(nblk)], axis=0
    )
    out = jnp.dot(w_ref[...], xm, preferred_element_type=jnp.float32)
    rows = 2 * p_chunk * share
    own_ref[...] = out[:rows].reshape(own_ref.shape)
    send_ref[...] = out[rows:].astype(jnp.bfloat16).reshape(send_ref.shape)


def half_chunk(chunk, scal, occ_all, pair_mask, flat, fit_dev, share):
    p_chunk = fit_dev // CHUNKS
    rows, nu = flat.shape
    nblk = rows // (BLK * fit_dev)
    out_rows = 2 * p_chunk * share
    return pl.pallas_call(
        functools.partial(half_kernel, chunk, p_chunk, fit_dev, share),
        grid_spec=pltpu.PrefetchScalarGridSpec(
            num_scalar_prefetch=1,
            grid=(nu // TILE,),
            in_specs=[
                pl.BlockSpec(occ_all.shape, lambda j, s: (0, 0)),
                pl.BlockSpec(pair_mask.shape, lambda j, s: (0, 0)),
                pl.BlockSpec((rows, TILE), lambda j, s: (0, j)),
            ],
            out_specs=[
                pl.BlockSpec((out_rows, TILE), lambda j, s: (0, j)),
                pl.BlockSpec((out_rows, TILE), lambda j, s: (0, j)),
            ],
            scratch_shapes=[
                pltpu.VMEM((2 * out_rows, rows), jnp.bfloat16),
                pltpu.VMEM((nblk, pair_mask.shape[1]), jnp.float32),
            ],
        ),
        out_shape=[
            jax.ShapeDtypeStruct((out_rows, nu), jnp.float32),
            jax.ShapeDtypeStruct((out_rows, nu), jnp.bfloat16),
        ],
        compiler_params=pltpu.CompilerParams(vmem_limit_bytes=32 * 2**20),
        cost_estimate=pl.CostEstimate(
            flops=2 * 2 * out_rows * rows * nu, bytes_accessed=rows * nu * 2 + out_rows * nu * 6, transcendentals=0
        ),
        name="half_chunk",
    )(scal, occ_all, pair_mask, flat)


def project_kernel(n_h, idx, *refs):
    h_refs, vir_ref, out_ref = refs[:n_h], refs[n_h], refs[-1]
    which = pl.program_id(0)
    for k in range(n_h):

        @pl.when(which == k)
        def _(k=k):
            out_ref[...] = jnp.dot(
                h_refs[k][...], vir_ref[...], preferred_element_type=jnp.float32
            ).astype(jnp.bfloat16)


def project(out, idx, hs, vir, total_rows):
    rows, nu = hs[0].shape
    nv = vir.shape[1]
    n_h = len(hs)
    ops = [idx, *hs, vir] + ([] if out is None else [out])
    return pl.pallas_call(
        functools.partial(project_kernel, n_h),
        grid_spec=pltpu.PrefetchScalarGridSpec(
            num_scalar_prefetch=1,
            grid=(n_h,),
            in_specs=[pl.BlockSpec((rows, nu), lambda g, s: (0, 0)) for _ in hs]
            + [pl.BlockSpec(vir.shape, lambda g, s: (0, 0))]
            + ([] if out is None else [pl.BlockSpec(memory_space=pl.ANY)]),
            out_specs=pl.BlockSpec((rows, nv), lambda g, s: (s[g], 0)),
        ),
        out_shape=jax.ShapeDtypeStruct((total_rows, nv), jnp.bfloat16),
        input_output_aliases={} if out is None else {len(ops) - 1: 0},
        compiler_params=pltpu.CompilerParams(vmem_limit_bytes=32 * 2**20),
        cost_estimate=pl.CostEstimate(
            flops=2 * n_h * rows * nu * nv, bytes_accessed=n_h * rows * (nu + nv) * 2 + nu * nv * 2, transcendentals=0
        ),
        name="project",
    )(*ops)


def shards_blocked(integrals, pair_mask, row_blocks, occ_coef, vir_coef):
    mu_dev, fit_dev, nu = integrals.shape
    nocc = occ_coef.shape[1]
    nbas, nfit = lax.axis_size("basis"), lax.axis_size("fit")
    share = nocc // nbas
    nblk = mu_dev // BLK
    p_chunk = fit_dev // CHUNKS
    me = lax.axis_index("basis")
    x, c = me // 2, me % 2
    f = lax.axis_index("fit")
    z, y = f // YS, f % YS

    pair = lax.ppermute(occ_coef, "basis", CORE_SWAP)
    two = jnp.where(c == 0, jnp.concatenate([occ_coef, pair]), jnp.concatenate([pair, occ_coef]))
    far = lax.ppermute(two, "basis", X_SWAP)
    occ_all = jnp.where(x == 0, jnp.concatenate([two, far]), jnp.concatenate([far, two]))

    owned = lax.dynamic_slice_in_dim(row_blocks, me * nblk, nblk)
    dest = jnp.arange(nbas, dtype=jnp.int32)
    place = (dest // 2 != x).astype(jnp.int32) + 2 * (dest % 2 != c).astype(jnp.int32)
    scal = jnp.concatenate([place, owned.astype(jnp.int32)])
    flat = integrals.reshape(mu_dev * fit_dev, nu)

    halves = []
    for k in range(CHUNKS):
        own, send = half_chunk(k, scal, occ_all, pair_mask, flat, fit_dev, share)
        n = p_chunk * share
        got = lax.ppermute(send, "basis", CORE_SWAP)
        to_x = (own[n:] + got[n:].astype(jnp.float32)).astype(jnp.bfloat16)
        from_x = lax.ppermute(to_x, "basis", X_SWAP)
        halves.append((own[:n] + got[:n].astype(jnp.float32) + from_x.astype(jnp.float32)).astype(jnp.bfloat16))

    total = nfit * fit_dev * share
    out = None
    held = list(halves)
    for s in range(ZS):
        for k in range(CHUNKS):
            src_z = (z - s) % ZS
            other = lax.ppermute(held[k], "fit", Y_SWAP)
            idx = jnp.stack([(src_z * YS + y) * CHUNKS + k, (src_z * YS + 1 - y) * CHUNKS + k]).astype(jnp.int32)
            out = project(out, idx, [held[k], other], vir_coef, total)
            if s < ZS - 1:
                held[k] = lax.ppermute(held[k], "fit", Z_RING)
    return out.reshape(nfit * fit_dev, share, vir_coef.shape[1])


def shards(integrals, pair_mask, row_blocks, occ_coef, vir_coef):
    mu_dev = integrals.shape[0]
    fit_dev = integrals.shape[1]
    width_nu = integrals.shape[2]
    nocc = occ_coef.shape[1]
    blocks_dev = mu_dev // BLK
    owned = lax.dynamic_slice_in_dim(row_blocks, lax.axis_index("basis") * blocks_dev, blocks_dev)
    panels = lax.all_gather(occ_coef, "basis", axis=0, tiled=True)
    panel_blocks = panels.reshape(-1, BLK, nocc)
    mask_rows = jnp.take(pair_mask, owned, axis=0).astype(jnp.bfloat16)
    mask_full = jnp.repeat(jnp.repeat(mask_rows, BLK, axis=0), BLK, axis=1)
    masked = integrals * mask_full[:, None, :]
    share = nocc // lax.axis_size("basis")
    occ_rows = jnp.take(panel_blocks, owned, axis=0).reshape(mu_dev, nocc)
    flat = masked.reshape(mu_dev, fit_dev * width_nu)
    summed = lax.psum_scatter(
        lax.dot_general(
            occ_rows, flat, (((0,), (0,)), ((), ())), preferred_element_type=jnp.float32
        ),
        "basis",
        scatter_dimension=0,
        tiled=True,
    )
    half = summed.astype(jnp.bfloat16).reshape(share, fit_dev, width_nu)
    product = jnp.einsum(
        "ipn,na->pia",
        lax.all_gather(half, "fit", axis=1, tiled=True),
        vir_coef,
        preferred_element_type=jnp.float32,
    )
    return product.astype(jnp.bfloat16)


def solution(mesh):
    placed = (P("basis", "fit", None), P(), P(), P("basis", None), P(None, "fit"))
    body = shards_blocked if (mesh.shape["basis"], mesh.shape["fit"]) == (4, ZS * YS) else shards
    return jax.shard_map(body, mesh=mesh, in_specs=placed, out_specs=P(None, "basis", "fit"), check_vma=False)
```

```python
import functools

import jax
import jax.numpy as jnp
from jax import lax
from jax.experimental import pallas as pl
from jax.experimental.pallas import tpu as pltpu
from jax.sharding import PartitionSpec as P

BLK = 16
CHUNKS = 2
ZS, YS = 4, 2

CORE_SWAP = [(0, 1), (1, 0), (2, 3), (3, 2)]
X_SWAP = [(0, 2), (2, 0), (1, 3), (3, 1)]
DIAGONAL = [(0, 3), (3, 0), (1, 2), (2, 1)]
Y_SWAP = [(f, f ^ 1) for f in range(ZS * YS)]
Z_RING = [(f, (f + YS) % (ZS * YS)) for f in range(ZS * YS)]

IN_ANY = pl.BlockSpec(memory_space=pl.ANY)
IN_VMEM = pl.BlockSpec(memory_space=pltpu.VMEM)
IN_SMEM = pl.BlockSpec(memory_space=pltpu.SMEM)


def params():
    return pltpu.CompilerParams(vmem_limit_bytes=16 * 2**20)


def vmem(value):
    return pltpu.with_memory_space_constraint(value, pltpu.VMEM)


def order_kernel(me, row_blocks, mask_ref, flat_ref, out_ref, x_ref, sems):
    rows, nu = x_ref.shape
    fit_dev = out_ref.shape[0]
    depth = BLK * fit_dev
    nblk = rows // depth
    nnb = mask_ref.shape[1]
    copies = [
        pltpu.make_async_copy(
            flat_ref.at[pl.ds(b * depth, depth)], x_ref.at[pl.ds(b * depth, depth)], sems.at[b]
        )
        for b in range(nblk)
    ]
    for copy in copies:
        copy.start()
    to = lax.broadcasted_iota(jnp.int32, (depth, depth), 0)
    at = lax.broadcasted_iota(jnp.int32, (depth, depth), 1)
    turn = jnp.where((to // BLK == at % fit_dev) & (to % BLK == at // fit_dev), 1.0, 0.0).astype(jnp.bfloat16)
    column = lax.broadcasted_iota(jnp.int32, (nnb, nu), 1) // BLK
    block = lax.broadcasted_iota(jnp.int32, (nnb, nu), 0)
    widen = jnp.where(column == block, 1.0, 0.0).astype(jnp.bfloat16)
    owned = jnp.concatenate(
        [mask_ref[pl.ds(row_blocks[me[0] * nblk + b], 1), :] for b in range(nblk)], axis=0
    )
    mask = jnp.dot(owned.astype(jnp.float32).astype(jnp.bfloat16), widen, preferred_element_type=jnp.float32)
    for b in range(nblk):
        copies[b].wait()
        masked = x_ref[b * depth : (b + 1) * depth, :] * mask[b : b + 1, :].astype(jnp.bfloat16)
        turned = jnp.dot(turn, masked, preferred_element_type=jnp.float32).astype(jnp.bfloat16)
        out_ref[:, b * BLK : (b + 1) * BLK, :] = turned.reshape(fit_dev, BLK, nu)


def order(me, row_blocks, pair_mask, integrals):
    mu_dev, fit_dev, nu = integrals.shape
    rows = mu_dev * fit_dev
    nblk = mu_dev // BLK
    return pl.pallas_call(
        order_kernel,
        in_specs=[IN_SMEM, IN_SMEM, IN_VMEM, IN_ANY],
        out_specs=IN_VMEM,
        scratch_shapes=[pltpu.VMEM((rows, nu), jnp.bfloat16), pltpu.SemaphoreType.DMA((nblk,))],
        out_shape=pltpu.VMEM((fit_dev, mu_dev, nu), jnp.bfloat16),
        compiler_params=params(),
        cost_estimate=pl.CostEstimate(
            flops=2 * rows * BLK * fit_dev * nu, bytes_accessed=rows * nu * 4, transcendentals=0
        ),
        name="order",
    )(me, row_blocks, pair_mask, pltpu.with_memory_space_constraint(integrals.reshape(rows, nu), pltpu.HBM))


def half_kernel(start, me_ref, row_blocks, own_occ, far_occ, core_occ, diag_occ, x_ref, own_ref, send_ref, occ_ref):
    me = me_ref[0]
    rows, nocc = own_occ.shape
    nblk = rows // BLK
    share = nocc // 4
    x, c = me // 2, me % 2
    device = [me, 2 * (1 - x) + c, 2 * x + 1 - c, 2 * (1 - x) + 1 - c]
    for k, occ in enumerate((own_occ, far_occ, core_occ, diag_occ)):
        occ_ref[pl.ds(pl.multiple_of(device[k] * rows, rows), rows), :] = occ[...]
    to = lax.broadcasted_iota(jnp.int32, (nocc, nocc), 0)
    at = lax.broadcasted_iota(jnp.int32, (nocc, nocc), 1)
    dest = jnp.full((nocc, nocc), device[3], jnp.int32)
    for k in range(3):
        dest = jnp.where(to // share == k, device[k], dest)
    pick = jnp.where((at // share == dest) & (at % share == to % share), 1.0, 0.0).astype(jnp.bfloat16)
    mine = jnp.concatenate(
        [occ_ref[pl.ds(pl.multiple_of(row_blocks[me * nblk + b] * BLK, BLK), BLK), :] for b in range(nblk)], axis=0
    )
    turned = lax.dot_general(pick, mine, (((1,), (1,)), ((), ())), preferred_element_type=jnp.float32)
    turned = turned.astype(jnp.bfloat16)
    zero = jnp.zeros_like(turned)
    pair = jnp.concatenate(
        [jnp.concatenate([turned, zero], axis=1), jnp.concatenate([zero, turned], axis=1)], axis=0
    )
    for u in range(0, own_ref.shape[1], 2):
        both = x_ref[start + u : start + u + 2].reshape(2 * rows, x_ref.shape[2])
        out = jnp.dot(pair, both, preferred_element_type=jnp.float32)
        for v in range(2):
            for k in range(2):
                at_own, at_send = v * nocc + k * share, v * nocc + (2 + k) * share
                own_ref[k, u + v] = out[at_own : at_own + share]
                send_ref[k, u + v] = out[at_send : at_send + share].astype(jnp.bfloat16)


def half_terms(me, row_blocks, occs, turned, start, count):
    _, rows, nu = turned.shape
    nocc = occs[0].shape[1]
    share = nocc // 4
    return pl.pallas_call(
        functools.partial(half_kernel, start),
        in_specs=[IN_SMEM, IN_SMEM] + [IN_VMEM] * 5,
        out_specs=[IN_VMEM] * 2,
        scratch_shapes=[pltpu.VMEM((4 * rows, nocc), jnp.bfloat16)],
        out_shape=[
            pltpu.VMEM((2, count, share, nu), jnp.float32),
            pltpu.VMEM((2, count, share, nu), jnp.bfloat16),
        ],
        compiler_params=params(),
        cost_estimate=pl.CostEstimate(
            flops=4 * count * nocc * rows * nu, bytes_accessed=count * nu * (2 * rows + 3 * nocc), transcendentals=0
        ),
        name="half",
    )(me, row_blocks, *[vmem(occ) for occ in occs], vmem(turned))


def project_kernel(chunk, place, a_ref, b_ref, vir_ref, *refs):
    out_ref, buf, sems = refs[-4], refs[-2], refs[-1]
    rows, nv = a_ref.shape[0], vir_ref.shape[1]
    z, y = place[0], place[1]
    both = jnp.concatenate([a_ref[...], b_ref[...]], axis=0)
    copies = []
    for j in range(2):
        cols = pl.ds(j * (nv // 2), nv // 2)
        buf[:, cols] = jnp.dot(both, vir_ref[:, cols], preferred_element_type=jnp.float32).astype(jnp.bfloat16)
        for v, to in enumerate((y, 1 - y)):
            copies.append(
                pltpu.make_async_copy(
                    buf.at[pl.ds(v * rows, rows), cols], out_ref.at[z, to, chunk, :, cols], sems.at[2 * j + v]
                )
            )
            copies[-1].start()
    for copy in copies:
        copy.wait()


def project(out, place, chunk, own, other, vir, passing):
    rows, nu = own.shape
    nv = vir.shape[1]
    first = out is None
    ops = [place, vmem(own), vmem(other), vmem(vir)] + ([] if first else [out]) + [passing]
    where = len(ops) - 1
    out_type = jax.ShapeDtypeStruct((ZS, YS, CHUNKS, rows, nv), jnp.bfloat16)
    return pl.pallas_call(
        functools.partial(project_kernel, chunk),
        in_specs=[IN_SMEM] + [IN_VMEM] * 3 + [IN_ANY] * (1 if first else 2),
        out_specs=[IN_ANY] * 2,
        scratch_shapes=[pltpu.VMEM((2 * rows, nv), jnp.bfloat16), pltpu.SemaphoreType.DMA((4,))],
        out_shape=[out_type, jax.ShapeDtypeStruct(passing.shape, passing.dtype)],
        input_output_aliases={where: 1} if first else {where - 1: 0, where: 1},
        compiler_params=params(),
        cost_estimate=pl.CostEstimate(
            flops=4 * rows * nu * nv, bytes_accessed=4 * rows * (nu + nv) + nu * nv * 2, transcendentals=0
        ),
        name="project",
    )(*ops)


def shards_blocked(integrals, pair_mask, row_blocks, occ_coef, vir_coef):
    mu_dev, fit_dev, nu = integrals.shape
    nocc = occ_coef.shape[1]
    share = nocc // 4
    count = fit_dev // CHUNKS
    me = lax.axis_index("basis").astype(jnp.int32).reshape(1)
    f = lax.axis_index("fit")
    z, y = f // YS, f % YS

    occs = [occ_coef] + [lax.ppermute(occ_coef, "basis", swap) for swap in (X_SWAP, CORE_SWAP, DIAGONAL)]
    turned = order(me, row_blocks, pair_mask, integrals)

    held = []
    for k in range(CHUNKS):
        own, send = half_terms(me, row_blocks, occs, turned, k * count, count)
        got = lax.ppermute(send, "basis", CORE_SWAP)
        to_x = (own[1] + got[1].astype(jnp.float32)).astype(jnp.bfloat16)
        from_x = lax.ppermute(to_x, "basis", X_SWAP)
        total = own[0] + got[0].astype(jnp.float32) + from_x.astype(jnp.float32)
        held.append(total.astype(jnp.bfloat16).reshape(count * share, nu))

    out = None
    for s in range(ZS):
        for k in range(CHUNKS):
            other = lax.ppermute(held[k], "fit", Y_SWAP)
            coming = lax.ppermute(held[k], "fit", Z_RING) if s < ZS - 1 else me
            place = jnp.stack([(z - s) % ZS, y]).astype(jnp.int32)
            out, held[k] = project(out, place, k, held[k], other, vir_coef, coming)
    return out.reshape(ZS * YS * fit_dev, share, vir_coef.shape[1])


def shards(integrals, pair_mask, row_blocks, occ_coef, vir_coef):
    mu_dev = integrals.shape[0]
    fit_dev = integrals.shape[1]
    width_nu = integrals.shape[2]
    nocc = occ_coef.shape[1]
    blocks_dev = mu_dev // BLK
    owned = lax.dynamic_slice_in_dim(row_blocks, lax.axis_index("basis") * blocks_dev, blocks_dev)
    panels = lax.all_gather(occ_coef, "basis", axis=0, tiled=True)
    panel_blocks = panels.reshape(-1, BLK, nocc)
    mask_rows = jnp.take(pair_mask, owned, axis=0).astype(jnp.bfloat16)
    mask_full = jnp.repeat(jnp.repeat(mask_rows, BLK, axis=0), BLK, axis=1)
    masked = integrals * mask_full[:, None, :]
    share = nocc // lax.axis_size("basis")
    occ_rows = jnp.take(panel_blocks, owned, axis=0).reshape(mu_dev, nocc)
    flat = masked.reshape(mu_dev, fit_dev * width_nu)
    summed = lax.psum_scatter(
        lax.dot_general(
            occ_rows, flat, (((0,), (0,)), ((), ())), preferred_element_type=jnp.float32
        ),
        "basis",
        scatter_dimension=0,
        tiled=True,
    )
    half = summed.astype(jnp.bfloat16).reshape(share, fit_dev, width_nu)
    product = jnp.einsum(
        "ipn,na->pia",
        lax.all_gather(half, "fit", axis=1, tiled=True),
        vir_coef,
        preferred_element_type=jnp.float32,
    )
    return product.astype(jnp.bfloat16)


def solution(mesh):
    placed = (P("basis", "fit", None), P(), P(), P("basis", None), P(None, "fit"))
    body = shards_blocked if (mesh.shape["basis"], mesh.shape["fit"]) == (4, ZS * YS) else shards
    return jax.shard_map(body, mesh=mesh, in_specs=placed, out_specs=P(None, "basis", "fit"), check_vma=False)
```

```python
import functools

import jax
import jax.numpy as jnp
from jax import lax
from jax.experimental import pallas as pl
from jax.experimental.pallas import tpu as pltpu
from jax.sharding import PartitionSpec as P

BLK = 16
GROUPS = 2
PARTS = (8, 8)
ZS, YS = 4, 2
PROJ_FLOPS = 1000
PROJ_BYTES = 1000

CORE_SWAP = [(0, 1), (1, 0), (2, 3), (3, 2)]
X_SWAP = [(0, 2), (2, 0), (1, 3), (3, 1)]
DIAGONAL = [(0, 3), (3, 0), (1, 2), (2, 1)]
Y_SWAP = [(f, f ^ 1) for f in range(ZS * YS)]
Z_RING = [(f, (f + YS) % (ZS * YS)) for f in range(ZS * YS)]
Z_BACK = [(to, f) for f, to in Z_RING]

IN_ANY = pl.BlockSpec(memory_space=pl.ANY)
IN_VMEM = pl.BlockSpec(memory_space=pltpu.VMEM)
IN_SMEM = pl.BlockSpec(memory_space=pltpu.SMEM)


def params():
    return pltpu.CompilerParams(vmem_limit_bytes=16 * 2**20)


def vmem(value):
    return pltpu.with_memory_space_constraint(value, pltpu.VMEM)


def hbm(value):
    return pltpu.with_memory_space_constraint(value, pltpu.HBM)


def turn_blocks(x_ref, out_ref, first_p, blocks):
    count, mu_dev, nu = out_ref.shape
    depth = x_ref.shape[0] // (mu_dev // BLK)
    fit_dev = depth // BLK
    to = lax.broadcasted_iota(jnp.int32, (count * BLK, depth), 0)
    at = lax.broadcasted_iota(jnp.int32, (count * BLK, depth), 1)
    same = (to // BLK + first_p == at % fit_dev) & (to % BLK == at // fit_dev)
    turn = jnp.where(same, 1.0, 0.0).astype(jnp.bfloat16)
    for b in blocks:
        block = x_ref[b * depth : (b + 1) * depth, :]
        turned = jnp.dot(turn, block, preferred_element_type=jnp.float32).astype(jnp.bfloat16)
        out_ref[:, b * BLK : (b + 1) * BLK, :] = turned.reshape(count, BLK, nu)


def first_kernel(me, row_blocks_hbm, mask_hbm, flat_hbm, vir_hbm, out_ref, row_blocks, vir_ref, x_ref, mask_ref, sems):
    rows, nu = x_ref.shape
    nblk = out_ref.shape[1] // BLK
    depth = rows // nblk
    nnb = mask_ref.shape[1]
    small = [
        pltpu.make_async_copy(row_blocks_hbm, row_blocks, sems.at[GROUPS]),
        pltpu.make_async_copy(mask_hbm, mask_ref, sems.at[GROUPS + 1]),
    ]
    part = rows // GROUPS
    copies = [
        pltpu.make_async_copy(flat_hbm.at[pl.ds(g * part, part)], x_ref.at[pl.ds(g * part, part)], sems.at[g])
        for g in range(GROUPS)
    ]
    vir_copy = pltpu.make_async_copy(vir_hbm, vir_ref, sems.at[GROUPS + 2])
    for copy in (*small, *copies, vir_copy):
        copy.start()
    column = lax.broadcasted_iota(jnp.int32, (nnb, nu), 1) // BLK
    block = lax.broadcasted_iota(jnp.int32, (nnb, nu), 0)
    widen = jnp.where(column == block, 1.0, 0.0).astype(jnp.bfloat16)
    for copy in small:
        copy.wait()
    owned = jnp.concatenate(
        [mask_ref[pl.ds(row_blocks[me[0] * nblk + b], 1), :] for b in range(nblk)], axis=0
    )
    mask = jnp.dot(owned.astype(jnp.float32).astype(jnp.bfloat16), widen, preferred_element_type=jnp.float32)
    mask = mask.astype(jnp.bfloat16)
    for g in range(GROUPS):
        copies[g].wait()
        blocks = range(g * nblk // GROUPS, (g + 1) * nblk // GROUPS)
        for b in blocks:
            x_ref[b * depth : (b + 1) * depth, :] *= mask[b : b + 1, :]
        turn_blocks(x_ref, out_ref, 0, blocks)
    vir_copy.wait()


def first_order(me, row_blocks, pair_mask, integrals, vir, count):
    mu_dev, fit_dev, nu = integrals.shape
    rows = mu_dev * fit_dev
    return pl.pallas_call(
        first_kernel,
        in_specs=[IN_SMEM] + [IN_ANY] * 4,
        out_specs=[IN_VMEM, IN_SMEM, IN_VMEM, IN_VMEM],
        scratch_shapes=[
            pltpu.VMEM(pair_mask.shape, jnp.int32),
            pltpu.SemaphoreType.DMA((GROUPS + 3,)),
        ],
        out_shape=[
            pltpu.VMEM((count, mu_dev, nu), jnp.bfloat16),
            pltpu.SMEM(row_blocks.shape, jnp.int32),
            pltpu.VMEM(vir.shape, vir.dtype),
            pltpu.VMEM((rows, nu), jnp.bfloat16),
        ],
        compiler_params=params(),
        cost_estimate=pl.CostEstimate(
            flops=2 * rows * BLK * count * nu, bytes_accessed=rows * nu * 4, transcendentals=0
        ),
        name="order",
    )(me, hbm(row_blocks), hbm(pair_mask), hbm(integrals.reshape(rows, nu)), hbm(vir))


def next_kernel(first_p, x_ref, out_ref):
    turn_blocks(x_ref, out_ref, first_p, range(out_ref.shape[1] // BLK))


def next_order(masked, first_p, count, mu_dev):
    rows, nu = masked.shape
    return pl.pallas_call(
        functools.partial(next_kernel, first_p),
        in_specs=[IN_VMEM],
        out_specs=IN_VMEM,
        out_shape=pltpu.VMEM((count, mu_dev, nu), jnp.bfloat16),
        compiler_params=params(),
        cost_estimate=pl.CostEstimate(
            flops=2 * rows * BLK * count * nu, bytes_accessed=rows * nu * 4, transcendentals=0
        ),
        name="order",
    )(vmem(masked))


def half_kernel(me_ref, row_blocks, own_occ, far_occ, core_occ, diag_occ, x_ref, here_ref, far_ref, send_ref):
    me = me_ref[0]
    nocc, rows = own_occ.shape
    nblk = rows // BLK
    share = nocc // 4
    x, c = me // 2, me % 2
    device = [me, 2 * (1 - x) + c, 2 * x + 1 - c, 2 * (1 - x) + 1 - c]
    lane = lax.broadcasted_iota(jnp.int32, (rows, rows), 1)
    wanted = jnp.zeros((rows, rows), jnp.int32)
    for b in range(nblk):
        wanted = jnp.where(lane // BLK == b, row_blocks[me * nblk + b] * BLK + lane % BLK, wanted)
    held = lax.broadcasted_iota(jnp.int32, (rows, rows), 0)
    mine = jnp.zeros((nocc, rows), jnp.float32)
    for k, occ in enumerate((own_occ, far_occ, core_occ, diag_occ)):
        take = jnp.where(held + device[k] * rows == wanted, 1.0, 0.0).astype(jnp.bfloat16)
        mine += jnp.dot(occ[...], take, preferred_element_type=jnp.float32)
    to = lax.broadcasted_iota(jnp.int32, (nocc, nocc), 0)
    at = lax.broadcasted_iota(jnp.int32, (nocc, nocc), 1)
    dest = jnp.full((nocc, nocc), device[3], jnp.int32)
    for k in range(3):
        dest = jnp.where(to // share == k, device[k], dest)
    pick = jnp.where((at // share == dest) & (at % share == to % share), 1.0, 0.0).astype(jnp.bfloat16)
    turned = jnp.dot(pick, mine.astype(jnp.bfloat16), preferred_element_type=jnp.float32).astype(jnp.bfloat16)
    zero = jnp.zeros_like(turned)
    pair = jnp.concatenate(
        [jnp.concatenate([turned, zero], axis=1), jnp.concatenate([zero, turned], axis=1)], axis=0
    )
    for u in range(0, here_ref.shape[0], 2):
        both = x_ref[u : u + 2].reshape(2 * rows, x_ref.shape[2])
        out = jnp.dot(pair, both, preferred_element_type=jnp.float32)
        for v in range(2):
            for k, own_ref in enumerate((here_ref, far_ref)):
                at_own, at_send = v * nocc + k * share, v * nocc + (2 + k) * share
                own_ref[u + v] = out[at_own : at_own + share]
                send_ref[k, u + v] = out[at_send : at_send + share].astype(jnp.bfloat16)


def half_terms(me, row_blocks, occs, turned):
    count, rows, nu = turned.shape
    nocc = occs[0].shape[0]
    share = nocc // 4
    return pl.pallas_call(
        half_kernel,
        in_specs=[IN_SMEM, IN_SMEM] + [IN_VMEM] * 5,
        out_specs=[IN_VMEM] * 3,
        out_shape=[
            pltpu.VMEM((count, share, nu), jnp.float32),
            pltpu.VMEM((count, share, nu), jnp.float32),
            pltpu.VMEM((2, count, share, nu), jnp.bfloat16),
        ],
        compiler_params=params(),
        cost_estimate=pl.CostEstimate(
            flops=4 * count * nocc * rows * nu, bytes_accessed=count * nu * (2 * rows + 3 * nocc), transcendentals=0
        ),
        name="half",
    )(me, row_blocks, *[vmem(occ) for occ in occs], vmem(turned))


def add_kernel(k, own_ref, core_ref, *refs):
    out_ref = refs[-1]
    total = own_ref[...] + core_ref[k].astype(jnp.float32)
    for ref in refs[:-1]:
        total += ref[...].astype(jnp.float32)
    out_ref[...] = total.astype(jnp.bfloat16).reshape(out_ref.shape)


def add(own, core, k, others, shape):
    return pl.pallas_call(
        functools.partial(add_kernel, k),
        in_specs=[IN_VMEM] * (2 + len(others)),
        out_specs=IN_VMEM,
        out_shape=pltpu.VMEM(shape, jnp.bfloat16),
        compiler_params=params(),
        cost_estimate=pl.CostEstimate(flops=2 * own.size, bytes_accessed=8 * own.size, transcendentals=0),
        name="add",
    )(*[vmem(value) for value in (own, core, *others)])


def work_kernel(moved, made, n_copy, n_after, last, *refs):
    refs = list(refs)
    place, vir_ref = refs[:2]
    at = 2 + n_copy
    next_refs, h_refs = refs[2:at], refs[at : at + len(made)]
    prev_ref = refs[at + len(made)] if moved else None
    sems = refs[-1]
    copy_refs = refs[len(refs) - 1 - n_copy : -1]
    buf_ref, out_ref = refs[-2 - n_copy], refs[-3 - n_copy]
    if last:
        buf_ref, out_ref = refs[-2], refs[-3]
    y = place[ZS]

    def copies(buf, blocks, base):
        rows = buf.shape[0] // len(blocks)
        return [
            pltpu.make_async_copy(
                buf.at[pl.ds(v * rows, rows)],
                out_ref.at[place[step], 1 - y if side else y, pl.ds(first_row, rows)],
                sems.at[base + v],
            )
            for v, (step, first_row, side) in enumerate(blocks)
        ]

    going = copies(prev_ref, moved, 0) if moved else []
    for copy in going:
        copy.start()
    for next_ref, copy_ref in zip(next_refs, copy_refs):
        copy_ref[...] = next_ref[...]
    rows = jnp.concatenate([h[...] for h in h_refs], axis=0)
    buf_ref[...] = jnp.dot(rows, vir_ref[...], preferred_element_type=jnp.float32).astype(jnp.bfloat16)
    if last:
        final = copies(buf_ref, made, 2)
        for copy in final:
            copy.start()
        going += final
    for copy in going:
        copy.wait()


def work(state, place, vir, made, hs, out_type, sent=(), after=(), last=False):
    out, buf, moved = state
    rows, nv = hs[0].shape[0], vir.shape[1]
    inside = [vir, *sent, *hs] + ([buf] if moved else [])
    ops = [place, *map(vmem, inside), *after] + ([] if out is None else [out])
    block = pltpu.VMEM((len(hs) * rows, nv), jnp.bfloat16)
    results = [] if last else [block] + [pltpu.VMEM(value.shape, value.dtype) for value in sent]
    got = pl.pallas_call(
        functools.partial(work_kernel, moved, made, len(sent), len(after), last),
        in_specs=[IN_SMEM] + [IN_VMEM] * len(inside) + [IN_ANY] * (len(after) + (out is not None)),
        out_specs=[IN_ANY] + [IN_VMEM] * len(results),
        scratch_shapes=([block] if last else []) + [pltpu.SemaphoreType.DMA((4,))],
        out_shape=[out_type] + results,
        input_output_aliases={} if out is None else {len(ops) - 1: 0},
        compiler_params=params(),
        cost_estimate=pl.CostEstimate(flops=PROJ_FLOPS, bytes_accessed=PROJ_BYTES, transcendentals=0),
        name="project",
    )(*ops)
    return (got[0], None if last else got[1], made), *got[2:]


def shards_blocked(integrals, pair_mask, row_blocks, occ_coef, vir_coef):
    mu_dev, fit_dev, nu = integrals.shape
    nocc, nv = occ_coef.shape[1], vir_coef.shape[1]
    share = nocc // 4
    me = lax.axis_index("basis").astype(jnp.int32).reshape(1)
    f = lax.axis_index("fit")
    z, y = f // YS, f % YS
    counts = [fit_dev * part // 16 for part in PARTS]
    starts = [0, counts[0]]

    occ = occ_coef.T
    occs = [occ] + [lax.ppermute(occ, "basis", swap) for swap in (X_SWAP, CORE_SWAP, DIAGONAL)]
    turned, row_blocks, vir, masked = first_order(me, row_blocks, pair_mask, integrals, vir_coef, counts[0])

    held = []
    for k in range(2):
        here, far, send = half_terms(me, row_blocks, occs, turned)
        got = lax.ppermute(send, "basis", CORE_SWAP)
        to_x = add(far, got, 1, [], far.shape)
        from_x = lax.ppermute(to_x, "basis", X_SWAP)
        held.append(add(here, got, 0, [from_x], (counts[k] * share, nu)))
        if k == 0:
            turned = next_order(masked, starts[1], counts[1], mu_dev)

    place = jnp.concatenate([(z - jnp.arange(ZS)) % ZS, y.reshape(1)]).astype(jnp.int32)
    run = functools.partial(
        work, place=place, vir=vir, out_type=jax.ShapeDtypeStruct((ZS, YS, fit_dev * share, nv), jnp.bfloat16)
    )
    up, down, swap = [functools.partial(lax.ppermute, axis_name="fit", perm=p) for p in (Z_RING, Z_BACK, Y_SWAP)]
    a0, b0 = held
    row_a, row_b = [start * share for start in starts]

    def pair(step, row):
        return [(step, row, 0), (step, row, 1)]

    a1, a0_y = up(a0), swap(a0)
    b1, b0_y = up(b0), swap(b0)
    a2 = up(a1)
    state, a1_copy = run((None, None, None), made=pair(0, row_a), hs=[a0, a0_y], sent=[a1])
    a1_y = swap(a1_copy)
    b2 = up(b1)
    state, b1_copy = run(state, made=pair(0, row_b), hs=[b0, b0_y], sent=[b1])
    b1_y = swap(b1_copy)
    a3 = up(a2)
    state, a2_copy = run(state, made=pair(1, row_a), hs=[a1, a1_y], sent=[a2])
    a2_y = swap(a2_copy)
    b3 = up(b2)
    state, b2_copy, b0_y_copy = run(state, made=pair(1, row_b), hs=[b1, b1_y], sent=[b2, b0_y])
    b2_y = swap(b2_copy)
    b3_y = down(b0_y_copy)
    state, a3_copy = run(state, made=pair(2, row_a), hs=[a2, a2_y], sent=[a3])
    a3_y = swap(a3_copy)
    state, = run(state, made=pair(2, row_b), hs=[b2, b2_y], after=[b3])
    state, = run(state, made=[(3, row_a, 0), (3, row_b, 0)], hs=[a3, b3])
    state, = run(state, made=[(3, row_a, 1)], hs=[a3_y])
    state, = run(state, made=[(3, row_b, 1)], hs=[b3_y], last=True)
    return state[0].reshape(ZS * YS * fit_dev, share, nv)


def shards(integrals, pair_mask, row_blocks, occ_coef, vir_coef):
    mu_dev = integrals.shape[0]
    fit_dev = integrals.shape[1]
    width_nu = integrals.shape[2]
    nocc = occ_coef.shape[1]
    blocks_dev = mu_dev // BLK
    owned = lax.dynamic_slice_in_dim(row_blocks, lax.axis_index("basis") * blocks_dev, blocks_dev)
    panels = lax.all_gather(occ_coef, "basis", axis=0, tiled=True)
    panel_blocks = panels.reshape(-1, BLK, nocc)
    mask_rows = jnp.take(pair_mask, owned, axis=0).astype(jnp.bfloat16)
    mask_full = jnp.repeat(jnp.repeat(mask_rows, BLK, axis=0), BLK, axis=1)
    masked = integrals * mask_full[:, None, :]
    share = nocc // lax.axis_size("basis")
    occ_rows = jnp.take(panel_blocks, owned, axis=0).reshape(mu_dev, nocc)
    flat = masked.reshape(mu_dev, fit_dev * width_nu)
    summed = lax.psum_scatter(
        lax.dot_general(
            occ_rows, flat, (((0,), (0,)), ((), ())), preferred_element_type=jnp.float32
        ),
        "basis",
        scatter_dimension=0,
        tiled=True,
    )
    half = summed.astype(jnp.bfloat16).reshape(share, fit_dev, width_nu)
    product = jnp.einsum(
        "ipn,na->pia",
        lax.all_gather(half, "fit", axis=1, tiled=True),
        vir_coef,
        preferred_element_type=jnp.float32,
    )
    return product.astype(jnp.bfloat16)


def solution(mesh):
    placed = (P("basis", "fit", None), P(), P(), P("basis", None), P(None, "fit"))
    body = shards_blocked if (mesh.shape["basis"], mesh.shape["fit"]) == (4, ZS * YS) else shards
    return jax.shard_map(body, mesh=mesh, in_specs=placed, out_specs=P(None, "basis", "fit"), check_vma=False)
```

```python
import functools

import jax
import jax.numpy as jnp
from jax import lax
from jax.experimental import pallas as pl
from jax.experimental.pallas import tpu as pltpu
from jax.sharding import PartitionSpec as P

BLK = 16
GROUPS = 2
PARTS = (8, 8)
ZS, YS = 4, 2
PROJ_FLOPS = 1000
PROJ_BYTES = 1000

CORE_SWAP = [(0, 1), (1, 0), (2, 3), (3, 2)]
X_SWAP = [(0, 2), (2, 0), (1, 3), (3, 1)]
DIAGONAL = [(0, 3), (3, 0), (1, 2), (2, 1)]
Y_SWAP = [(f, f ^ 1) for f in range(ZS * YS)]
Z_RING = [(f, (f + YS) % (ZS * YS)) for f in range(ZS * YS)]
Z_BACK = [(to, f) for f, to in Z_RING]

IN_ANY = pl.BlockSpec(memory_space=pl.ANY)
IN_VMEM = pl.BlockSpec(memory_space=pltpu.VMEM)
IN_SMEM = pl.BlockSpec(memory_space=pltpu.SMEM)


def params():
    return pltpu.CompilerParams(vmem_limit_bytes=16 * 2**20)


def vmem(value):
    return pltpu.with_memory_space_constraint(value, pltpu.VMEM)


def hbm(value):
    return pltpu.with_memory_space_constraint(value, pltpu.HBM)


def turn_blocks(x_ref, out_ref, first_p, blocks):
    count, mu_dev, nu = out_ref.shape
    depth = x_ref.shape[0] // (mu_dev // BLK)
    fit_dev = depth // BLK
    to = lax.broadcasted_iota(jnp.int32, (count * BLK, depth), 0)
    at = lax.broadcasted_iota(jnp.int32, (count * BLK, depth), 1)
    same = (to // BLK + first_p == at % fit_dev) & (to % BLK == at // fit_dev)
    turn = jnp.where(same, 1.0, 0.0).astype(jnp.bfloat16)
    for b in blocks:
        block = x_ref[b * depth : (b + 1) * depth, :]
        turned = jnp.dot(turn, block, preferred_element_type=jnp.float32).astype(jnp.bfloat16)
        out_ref[:, b * BLK : (b + 1) * BLK, :] = turned.reshape(count, BLK, nu)


def first_kernel(me, row_blocks_hbm, mask_hbm, flat_hbm, vir_hbm, out_ref, row_blocks, vir_ref, x_ref, mask_ref, sems):
    rows, nu = x_ref.shape
    nblk = out_ref.shape[1] // BLK
    depth = rows // nblk
    nnb = mask_ref.shape[1]
    small = [
        pltpu.make_async_copy(row_blocks_hbm, row_blocks, sems.at[GROUPS]),
        pltpu.make_async_copy(mask_hbm, mask_ref, sems.at[GROUPS + 1]),
    ]
    part = rows // GROUPS
    copies = [
        pltpu.make_async_copy(flat_hbm.at[pl.ds(g * part, part)], x_ref.at[pl.ds(g * part, part)], sems.at[g])
        for g in range(GROUPS)
    ]
    vir_copy = pltpu.make_async_copy(vir_hbm, vir_ref, sems.at[GROUPS + 2])
    for copy in (*small, *copies, vir_copy):
        copy.start()
    column = lax.broadcasted_iota(jnp.int32, (nnb, nu), 1) // BLK
    block = lax.broadcasted_iota(jnp.int32, (nnb, nu), 0)
    widen = jnp.where(column == block, 1.0, 0.0).astype(jnp.bfloat16)
    for copy in small:
        copy.wait()
    owned = jnp.concatenate(
        [mask_ref[pl.ds(row_blocks[me[0] * nblk + b], 1), :] for b in range(nblk)], axis=0
    )
    mask = jnp.dot(owned.astype(jnp.float32).astype(jnp.bfloat16), widen, preferred_element_type=jnp.float32)
    mask = mask.astype(jnp.bfloat16)
    for g in range(GROUPS):
        copies[g].wait()
        blocks = range(g * nblk // GROUPS, (g + 1) * nblk // GROUPS)
        for b in blocks:
            x_ref[b * depth : (b + 1) * depth, :] *= mask[b : b + 1, :]
        turn_blocks(x_ref, out_ref, 0, blocks)
    vir_copy.wait()


def first_order(me, row_blocks, pair_mask, integrals, vir, count):
    mu_dev, fit_dev, nu = integrals.shape
    rows = mu_dev * fit_dev
    return pl.pallas_call(
        first_kernel,
        in_specs=[IN_SMEM] + [IN_ANY] * 4,
        out_specs=[IN_VMEM, IN_SMEM, IN_VMEM, IN_VMEM],
        scratch_shapes=[
            pltpu.VMEM(pair_mask.shape, jnp.int32),
            pltpu.SemaphoreType.DMA((GROUPS + 3,)),
        ],
        out_shape=[
            pltpu.VMEM((count, mu_dev, nu), jnp.bfloat16),
            pltpu.SMEM(row_blocks.shape, jnp.int32),
            pltpu.VMEM(vir.shape, vir.dtype),
            pltpu.VMEM((rows, nu), jnp.bfloat16),
        ],
        compiler_params=params(),
        cost_estimate=pl.CostEstimate(
            flops=2 * rows * BLK * count * nu, bytes_accessed=rows * nu * 4, transcendentals=0
        ),
        name="order",
    )(me, hbm(row_blocks), hbm(pair_mask), hbm(integrals.reshape(rows, nu)), hbm(vir))


def next_kernel(first_p, x_ref, out_ref):
    turn_blocks(x_ref, out_ref, first_p, range(out_ref.shape[1] // BLK))


def next_order(masked, first_p, count, mu_dev):
    rows, nu = masked.shape
    return pl.pallas_call(
        functools.partial(next_kernel, first_p),
        in_specs=[IN_VMEM],
        out_specs=IN_VMEM,
        out_shape=pltpu.VMEM((count, mu_dev, nu), jnp.bfloat16),
        compiler_params=params(),
        cost_estimate=pl.CostEstimate(
            flops=2 * rows * BLK * count * nu, bytes_accessed=rows * nu * 4, transcendentals=0
        ),
        name="order",
    )(vmem(masked))


def half_kernel(me_ref, row_blocks, own_occ, far_occ, core_occ, diag_occ, x_ref, here_ref, far_ref, send_ref):
    me = me_ref[0]
    nocc, rows = own_occ.shape
    nblk = rows // BLK
    share = nocc // 4
    x, c = me // 2, me % 2
    device = [me, 2 * (1 - x) + c, 2 * x + 1 - c, 2 * (1 - x) + 1 - c]
    lane = lax.broadcasted_iota(jnp.int32, (rows, rows), 1)
    wanted = jnp.zeros((rows, rows), jnp.int32)
    for b in range(nblk):
        wanted = jnp.where(lane // BLK == b, row_blocks[me * nblk + b] * BLK + lane % BLK, wanted)
    held = lax.broadcasted_iota(jnp.int32, (rows, rows), 0)
    mine = jnp.zeros((nocc, rows), jnp.float32)
    for k, occ in enumerate((own_occ, far_occ, core_occ, diag_occ)):
        take = jnp.where(held + device[k] * rows == wanted, 1.0, 0.0).astype(jnp.bfloat16)
        mine += jnp.dot(occ[...], take, preferred_element_type=jnp.float32)
    to = lax.broadcasted_iota(jnp.int32, (nocc, nocc), 0)
    at = lax.broadcasted_iota(jnp.int32, (nocc, nocc), 1)
    dest = jnp.full((nocc, nocc), device[3], jnp.int32)
    for k in range(3):
        dest = jnp.where(to // share == k, device[k], dest)
    pick = jnp.where((at // share == dest) & (at % share == to % share), 1.0, 0.0).astype(jnp.bfloat16)
    turned = jnp.dot(pick, mine.astype(jnp.bfloat16), preferred_element_type=jnp.float32).astype(jnp.bfloat16)
    zero = jnp.zeros_like(turned)
    pair = jnp.concatenate(
        [jnp.concatenate([turned, zero], axis=1), jnp.concatenate([zero, turned], axis=1)], axis=0
    )
    for u in range(0, here_ref.shape[0], 2):
        both = x_ref[u : u + 2].reshape(2 * rows, x_ref.shape[2])
        out = jnp.dot(pair, both, preferred_element_type=jnp.float32)
        for v in range(2):
            for k, own_ref in enumerate((here_ref, far_ref)):
                at_own, at_send = v * nocc + k * share, v * nocc + (2 + k) * share
                own_ref[u + v] = out[at_own : at_own + share]
                send_ref[k, u + v] = out[at_send : at_send + share].astype(jnp.bfloat16)


def half_terms(me, row_blocks, occs, turned):
    count, rows, nu = turned.shape
    nocc = occs[0].shape[0]
    share = nocc // 4
    return pl.pallas_call(
        half_kernel,
        in_specs=[IN_SMEM, IN_SMEM] + [IN_VMEM] * 5,
        out_specs=[IN_VMEM] * 3,
        out_shape=[
            pltpu.VMEM((count, share, nu), jnp.float32),
            pltpu.VMEM((count, share, nu), jnp.float32),
            pltpu.VMEM((2, count, share, nu), jnp.bfloat16),
        ],
        compiler_params=params(),
        cost_estimate=pl.CostEstimate(
            flops=4 * count * nocc * rows * nu, bytes_accessed=count * nu * (2 * rows + 3 * nocc), transcendentals=0
        ),
        name="half",
    )(me, row_blocks, *[vmem(occ) for occ in occs], vmem(turned))


def meet_kernel(here_ref, far_ref, core_ref, sum_ref, send_ref):
    sum_ref[...] = here_ref[...] + core_ref[0].astype(jnp.float32)
    send_ref[...] = (far_ref[...] + core_ref[1].astype(jnp.float32)).astype(jnp.bfloat16)


def meet(here, far, core):
    return pl.pallas_call(
        meet_kernel,
        in_specs=[IN_VMEM] * 3,
        out_specs=[IN_VMEM] * 2,
        out_shape=[pltpu.VMEM(here.shape, jnp.float32), pltpu.VMEM(here.shape, jnp.bfloat16)],
        compiler_params=params(),
        cost_estimate=pl.CostEstimate(flops=2 * here.size, bytes_accessed=8 * here.size, transcendentals=0),
        name="meet",
    )(*map(vmem, (here, far, core)))


def finish_kernel(sum_ref, chip_ref, out_ref):
    total = sum_ref[...] + chip_ref[...].astype(jnp.float32)
    out_ref[...] = total.astype(jnp.bfloat16).reshape(out_ref.shape)


def finish(total, chip):
    count, share, nu = total.shape
    return pl.pallas_call(
        finish_kernel,
        in_specs=[IN_VMEM] * 2,
        out_specs=IN_VMEM,
        out_shape=pltpu.VMEM((count * share, nu), jnp.bfloat16),
        compiler_params=params(),
        cost_estimate=pl.CostEstimate(flops=2 * total.size, bytes_accessed=8 * total.size, transcendentals=0),
        name="finish",
    )(vmem(total), vmem(chip))


def work_kernel(moved, made, n_copy, n_after, last, *refs):
    refs = list(refs)
    place, vir_ref = refs[:2]
    at = 2 + n_copy
    next_refs, h_refs = refs[2:at], refs[at : at + len(made)]
    prev_ref = refs[at + len(made)] if moved else None
    sems = refs[-1]
    copy_refs = refs[len(refs) - 1 - n_copy : -1]
    buf_ref, out_ref = refs[-2 - n_copy], refs[-3 - n_copy]
    if last:
        buf_ref, out_ref = refs[-2], refs[-3]
    y = place[ZS]

    def copies(buf, blocks, base):
        rows = buf.shape[0] // len(blocks)
        return [
            pltpu.make_async_copy(
                buf.at[pl.ds(v * rows, rows)],
                out_ref.at[place[step], 1 - y if side else y, pl.ds(first_row, rows)],
                sems.at[base + v],
            )
            for v, (step, first_row, side) in enumerate(blocks)
        ]

    going = copies(prev_ref, moved, 0) if moved else []
    for copy in going:
        copy.start()
    for next_ref, copy_ref in zip(next_refs, copy_refs):
        copy_ref[...] = next_ref[...]
    rows = jnp.concatenate([h[...] for h in h_refs], axis=0)
    buf_ref[...] = jnp.dot(rows, vir_ref[...], preferred_element_type=jnp.float32).astype(jnp.bfloat16)
    if last:
        final = copies(buf_ref, made, 2)
        for copy in final:
            copy.start()
        going += final
    for copy in going:
        copy.wait()


def work(state, place, vir, made, hs, out_type, sent=(), after=(), last=False):
    out, buf, moved = state
    rows, nv = hs[0].shape[0], vir.shape[1]
    inside = [vir, *sent, *hs] + ([buf] if moved else [])
    ops = [place, *map(vmem, inside), *after] + ([] if out is None else [out])
    block = pltpu.VMEM((len(hs) * rows, nv), jnp.bfloat16)
    results = [] if last else [block] + [pltpu.VMEM(value.shape, value.dtype) for value in sent]
    got = pl.pallas_call(
        functools.partial(work_kernel, moved, made, len(sent), len(after), last),
        in_specs=[IN_SMEM] + [IN_VMEM] * len(inside) + [IN_ANY] * (len(after) + (out is not None)),
        out_specs=[IN_ANY] + [IN_VMEM] * len(results),
        scratch_shapes=([block] if last else []) + [pltpu.SemaphoreType.DMA((4,))],
        out_shape=[out_type] + results,
        input_output_aliases={} if out is None else {len(ops) - 1: 0},
        compiler_params=params(),
        cost_estimate=pl.CostEstimate(flops=PROJ_FLOPS, bytes_accessed=PROJ_BYTES, transcendentals=0),
        name="project",
    )(*ops)
    return (got[0], None if last else got[1], made), *got[2:]


def shards_blocked(integrals, pair_mask, row_blocks, occ_coef, vir_coef):
    mu_dev, fit_dev, nu = integrals.shape
    nocc, nv = occ_coef.shape[1], vir_coef.shape[1]
    share = nocc // 4
    me = lax.axis_index("basis").astype(jnp.int32).reshape(1)
    f = lax.axis_index("fit")
    z, y = f // YS, f % YS
    counts = [fit_dev * part // 16 for part in PARTS]
    starts = [0, counts[0]]

    occ = occ_coef.T
    occs = [occ] + [lax.ppermute(occ, "basis", swap) for swap in (X_SWAP, CORE_SWAP, DIAGONAL)]
    turned, row_blocks, vir, masked = first_order(me, row_blocks, pair_mask, integrals, vir_coef, counts[0])

    held = []
    for k in range(2):
        here, far, send = half_terms(me, row_blocks, occs, turned)
        total, to_x = meet(here, far, lax.ppermute(send, "basis", CORE_SWAP))
        held.append(finish(total, lax.ppermute(to_x, "basis", X_SWAP)))
        if k == 0:
            turned = next_order(masked, starts[1], counts[1], mu_dev)

    place = jnp.concatenate([(z - jnp.arange(ZS)) % ZS, y.reshape(1)]).astype(jnp.int32)
    run = functools.partial(
        work, place=place, vir=vir, out_type=jax.ShapeDtypeStruct((ZS, YS, fit_dev * share, nv), jnp.bfloat16)
    )
    up, down, swap = [functools.partial(lax.ppermute, axis_name="fit", perm=p) for p in (Z_RING, Z_BACK, Y_SWAP)]
    a0, b0 = held
    row_a, row_b = [start * share for start in starts]

    def pair(step, row):
        return [(step, row, 0), (step, row, 1)]

    a1, a0_y = up(a0), swap(a0)
    b1, b0_y = up(b0), swap(b0)
    a2 = up(a1)
    state, a1_copy = run((None, None, None), made=pair(0, row_a), hs=[a0, a0_y], sent=[a1])
    a1_y = swap(a1_copy)
    b2 = up(b1)
    state, b1_copy = run(state, made=pair(0, row_b), hs=[b0, b0_y], sent=[b1])
    b1_y = swap(b1_copy)
    a3 = up(a2)
    state, a2_copy = run(state, made=pair(1, row_a), hs=[a1, a1_y], sent=[a2])
    a2_y = swap(a2_copy)
    b3 = up(b2)
    state, b2_copy, b0_y_copy = run(state, made=pair(1, row_b), hs=[b1, b1_y], sent=[b2, b0_y])
    b2_y = swap(b2_copy)
    b3_y = down(b0_y_copy)
    state, a3_copy = run(state, made=pair(2, row_a), hs=[a2, a2_y], sent=[a3])
    a3_y = swap(a3_copy)
    state, = run(state, made=pair(2, row_b), hs=[b2, b2_y], after=[b3])
    state, = run(state, made=[(3, row_a, 0), (3, row_b, 0)], hs=[a3, b3])
    state, = run(state, made=[(3, row_a, 1)], hs=[a3_y])
    state, = run(state, made=[(3, row_b, 1)], hs=[b3_y], last=True)
    return state[0].reshape(ZS * YS * fit_dev, share, nv)


def shards(integrals, pair_mask, row_blocks, occ_coef, vir_coef):
    mu_dev = integrals.shape[0]
    fit_dev = integrals.shape[1]
    width_nu = integrals.shape[2]
    nocc = occ_coef.shape[1]
    blocks_dev = mu_dev // BLK
    owned = lax.dynamic_slice_in_dim(row_blocks, lax.axis_index("basis") * blocks_dev, blocks_dev)
    panels = lax.all_gather(occ_coef, "basis", axis=0, tiled=True)
    panel_blocks = panels.reshape(-1, BLK, nocc)
    mask_rows = jnp.take(pair_mask, owned, axis=0).astype(jnp.bfloat16)
    mask_full = jnp.repeat(jnp.repeat(mask_rows, BLK, axis=0), BLK, axis=1)
    masked = integrals * mask_full[:, None, :]
    share = nocc // lax.axis_size("basis")
    occ_rows = jnp.take(panel_blocks, owned, axis=0).reshape(mu_dev, nocc)
    flat = masked.reshape(mu_dev, fit_dev * width_nu)
    summed = lax.psum_scatter(
        lax.dot_general(
            occ_rows, flat, (((0,), (0,)), ((), ())), preferred_element_type=jnp.float32
        ),
        "basis",
        scatter_dimension=0,
        tiled=True,
    )
    half = summed.astype(jnp.bfloat16).reshape(share, fit_dev, width_nu)
    product = jnp.einsum(
        "ipn,na->pia",
        lax.all_gather(half, "fit", axis=1, tiled=True),
        vir_coef,
        preferred_element_type=jnp.float32,
    )
    return product.astype(jnp.bfloat16)


def solution(mesh):
    placed = (P("basis", "fit", None), P(), P(), P("basis", None), P(None, "fit"))
    body = shards_blocked if (mesh.shape["basis"], mesh.shape["fit"]) == (4, ZS * YS) else shards
    return jax.shard_map(body, mesh=mesh, in_specs=placed, out_specs=P(None, "basis", "fit"), check_vma=False)
```

```python
import functools

import jax
import jax.numpy as jnp
from jax import lax
from jax.experimental import pallas as pl
from jax.experimental.pallas import tpu as pltpu
from jax.sharding import PartitionSpec as P

BLK = 16
GROUPS = 2
PARTS = (8, 8)
ZS, YS = 4, 2
PROJ_FLOPS = 10**9
PROJ_BYTES = 1000

CORE_SWAP = [(0, 1), (1, 0), (2, 3), (3, 2)]
X_SWAP = [(0, 2), (2, 0), (1, 3), (3, 1)]
DIAGONAL = [(0, 3), (3, 0), (1, 2), (2, 1)]
Y_SWAP = [(f, f ^ 1) for f in range(ZS * YS)]
Z_RING = [(f, (f + YS) % (ZS * YS)) for f in range(ZS * YS)]
Z_BACK = [(to, f) for f, to in Z_RING]

IN_ANY = pl.BlockSpec(memory_space=pl.ANY)
IN_VMEM = pl.BlockSpec(memory_space=pltpu.VMEM)
IN_SMEM = pl.BlockSpec(memory_space=pltpu.SMEM)


def params():
    return pltpu.CompilerParams(vmem_limit_bytes=16 * 2**20)


def vmem(value):
    return pltpu.with_memory_space_constraint(value, pltpu.VMEM)


def hbm(value):
    return pltpu.with_memory_space_constraint(value, pltpu.HBM)


def turn_blocks(x_ref, out_ref, first_p, blocks):
    count, mu_dev, nu = out_ref.shape
    depth = x_ref.shape[0] // (mu_dev // BLK)
    fit_dev = depth // BLK
    to = lax.broadcasted_iota(jnp.int32, (count * BLK, depth), 0)
    at = lax.broadcasted_iota(jnp.int32, (count * BLK, depth), 1)
    same = (to // BLK + first_p == at % fit_dev) & (to % BLK == at // fit_dev)
    turn = jnp.where(same, 1.0, 0.0).astype(jnp.bfloat16)
    for b in blocks:
        block = x_ref[b * depth : (b + 1) * depth, :]
        turned = jnp.dot(turn, block, preferred_element_type=jnp.float32).astype(jnp.bfloat16)
        out_ref[:, b * BLK : (b + 1) * BLK, :] = turned.reshape(count, BLK, nu)


def first_kernel(me, row_blocks_hbm, mask_hbm, flat_hbm, vir_hbm, out_ref, row_blocks, vir_ref, x_ref, mask_ref, sems):
    rows, nu = x_ref.shape
    nblk = out_ref.shape[1] // BLK
    depth = rows // nblk
    nnb = mask_ref.shape[1]
    small = [
        pltpu.make_async_copy(row_blocks_hbm, row_blocks, sems.at[GROUPS]),
        pltpu.make_async_copy(mask_hbm, mask_ref, sems.at[GROUPS + 1]),
    ]
    part = rows // GROUPS
    copies = [
        pltpu.make_async_copy(flat_hbm.at[pl.ds(g * part, part)], x_ref.at[pl.ds(g * part, part)], sems.at[g])
        for g in range(GROUPS)
    ]
    vir_copy = pltpu.make_async_copy(vir_hbm, vir_ref, sems.at[GROUPS + 2])
    for copy in (*small, *copies, vir_copy):
        copy.start()
    column = lax.broadcasted_iota(jnp.int32, (nnb, nu), 1) // BLK
    block = lax.broadcasted_iota(jnp.int32, (nnb, nu), 0)
    widen = jnp.where(column == block, 1.0, 0.0).astype(jnp.bfloat16)
    for copy in small:
        copy.wait()
    owned = jnp.concatenate(
        [mask_ref[pl.ds(row_blocks[me[0] * nblk + b], 1), :] for b in range(nblk)], axis=0
    )
    mask = jnp.dot(owned.astype(jnp.float32).astype(jnp.bfloat16), widen, preferred_element_type=jnp.float32)
    mask = mask.astype(jnp.bfloat16)
    for g in range(GROUPS):
        copies[g].wait()
        blocks = range(g * nblk // GROUPS, (g + 1) * nblk // GROUPS)
        for b in blocks:
            x_ref[b * depth : (b + 1) * depth, :] *= mask[b : b + 1, :]
        turn_blocks(x_ref, out_ref, 0, blocks)
    vir_copy.wait()


def first_order(me, row_blocks, pair_mask, integrals, vir, count):
    mu_dev, fit_dev, nu = integrals.shape
    rows = mu_dev * fit_dev
    return pl.pallas_call(
        first_kernel,
        in_specs=[IN_SMEM] + [IN_ANY] * 4,
        out_specs=[IN_VMEM, IN_SMEM, IN_VMEM, IN_VMEM],
        scratch_shapes=[
            pltpu.VMEM(pair_mask.shape, jnp.int32),
            pltpu.SemaphoreType.DMA((GROUPS + 3,)),
        ],
        out_shape=[
            pltpu.VMEM((count, mu_dev, nu), jnp.bfloat16),
            pltpu.SMEM(row_blocks.shape, jnp.int32),
            pltpu.VMEM(vir.shape, vir.dtype),
            pltpu.VMEM((rows, nu), jnp.bfloat16),
        ],
        compiler_params=params(),
        cost_estimate=pl.CostEstimate(
            flops=2 * rows * BLK * count * nu, bytes_accessed=rows * nu * 4, transcendentals=0
        ),
        name="order",
    )(me, hbm(row_blocks), hbm(pair_mask), hbm(integrals.reshape(rows, nu)), hbm(vir))


def next_kernel(first_p, x_ref, out_ref):
    turn_blocks(x_ref, out_ref, first_p, range(out_ref.shape[1] // BLK))


def next_order(masked, first_p, count, mu_dev):
    rows, nu = masked.shape
    return pl.pallas_call(
        functools.partial(next_kernel, first_p),
        in_specs=[IN_VMEM],
        out_specs=IN_VMEM,
        out_shape=pltpu.VMEM((count, mu_dev, nu), jnp.bfloat16),
        compiler_params=params(),
        cost_estimate=pl.CostEstimate(
            flops=2 * rows * BLK * count * nu, bytes_accessed=rows * nu * 4, transcendentals=0
        ),
        name="order",
    )(vmem(masked))


def half_kernel(me_ref, row_blocks, own_occ, far_occ, core_occ, diag_occ, x_ref, here_ref, far_ref, send_ref):
    me = me_ref[0]
    nocc, rows = own_occ.shape
    nblk = rows // BLK
    share = nocc // 4
    x, c = me // 2, me % 2
    device = [me, 2 * (1 - x) + c, 2 * x + 1 - c, 2 * (1 - x) + 1 - c]
    lane = lax.broadcasted_iota(jnp.int32, (rows, rows), 1)
    wanted = jnp.zeros((rows, rows), jnp.int32)
    for b in range(nblk):
        wanted = jnp.where(lane // BLK == b, row_blocks[me * nblk + b] * BLK + lane % BLK, wanted)
    held = lax.broadcasted_iota(jnp.int32, (rows, rows), 0)
    mine = jnp.zeros((nocc, rows), jnp.float32)
    for k, occ in enumerate((own_occ, far_occ, core_occ, diag_occ)):
        take = jnp.where(held + device[k] * rows == wanted, 1.0, 0.0).astype(jnp.bfloat16)
        mine += jnp.dot(occ[...], take, preferred_element_type=jnp.float32)
    to = lax.broadcasted_iota(jnp.int32, (nocc, nocc), 0)
    at = lax.broadcasted_iota(jnp.int32, (nocc, nocc), 1)
    dest = jnp.full((nocc, nocc), device[3], jnp.int32)
    for k in range(3):
        dest = jnp.where(to // share == k, device[k], dest)
    pick = jnp.where((at // share == dest) & (at % share == to % share), 1.0, 0.0).astype(jnp.bfloat16)
    turned = jnp.dot(pick, mine.astype(jnp.bfloat16), preferred_element_type=jnp.float32).astype(jnp.bfloat16)
    zero = jnp.zeros_like(turned)
    pair = jnp.concatenate(
        [jnp.concatenate([turned, zero], axis=1), jnp.concatenate([zero, turned], axis=1)], axis=0
    )
    for u in range(0, here_ref.shape[0], 2):
        both = x_ref[u : u + 2].reshape(2 * rows, x_ref.shape[2])
        out = jnp.dot(pair, both, preferred_element_type=jnp.float32)
        for v in range(2):
            for k, own_ref in enumerate((here_ref, far_ref)):
                at_own, at_send = v * nocc + k * share, v * nocc + (2 + k) * share
                own_ref[u + v] = out[at_own : at_own + share]
                send_ref[k, u + v] = out[at_send : at_send + share].astype(jnp.bfloat16)


def half_terms(me, row_blocks, occs, turned):
    count, rows, nu = turned.shape
    nocc = occs[0].shape[0]
    share = nocc // 4
    return pl.pallas_call(
        half_kernel,
        in_specs=[IN_SMEM, IN_SMEM] + [IN_VMEM] * 5,
        out_specs=[IN_VMEM] * 3,
        out_shape=[
            pltpu.VMEM((count, share, nu), jnp.float32),
            pltpu.VMEM((count, share, nu), jnp.float32),
            pltpu.VMEM((2, count, share, nu), jnp.bfloat16),
        ],
        compiler_params=params(),
        cost_estimate=pl.CostEstimate(
            flops=4 * count * nocc * rows * nu, bytes_accessed=count * nu * (2 * rows + 3 * nocc), transcendentals=0
        ),
        name="half",
    )(me, row_blocks, *[vmem(occ) for occ in occs], vmem(turned))


def meet_kernel(here_ref, far_ref, core_ref, sum_ref, send_ref):
    sum_ref[...] = here_ref[...] + core_ref[0].astype(jnp.float32)
    send_ref[...] = (far_ref[...] + core_ref[1].astype(jnp.float32)).astype(jnp.bfloat16)


def meet(here, far, core):
    return pl.pallas_call(
        meet_kernel,
        in_specs=[IN_VMEM] * 3,
        out_specs=[IN_VMEM] * 2,
        out_shape=[pltpu.VMEM(here.shape, jnp.float32), pltpu.VMEM(here.shape, jnp.bfloat16)],
        compiler_params=params(),
        cost_estimate=pl.CostEstimate(flops=2 * here.size, bytes_accessed=8 * here.size, transcendentals=0),
        name="meet",
    )(*map(vmem, (here, far, core)))


def finish_kernel(sum_ref, chip_ref, out_ref):
    total = sum_ref[...] + chip_ref[...].astype(jnp.float32)
    out_ref[...] = total.astype(jnp.bfloat16).reshape(out_ref.shape)


def finish(total, chip):
    count, share, nu = total.shape
    return pl.pallas_call(
        finish_kernel,
        in_specs=[IN_VMEM] * 2,
        out_specs=IN_VMEM,
        out_shape=pltpu.VMEM((count * share, nu), jnp.bfloat16),
        compiler_params=params(),
        cost_estimate=pl.CostEstimate(flops=2 * total.size, bytes_accessed=8 * total.size, transcendentals=0),
        name="finish",
    )(vmem(total), vmem(chip))


def work_kernel(moved, made, n_copy, n_after, last, *refs):
    refs = list(refs)
    place, vir_ref = refs[:2]
    at = 2 + n_copy
    next_refs, h_refs = refs[2:at], refs[at : at + len(made)][::-1]
    prev_ref = refs[at + len(made)] if moved else None
    sems = refs[-1]
    copy_refs = refs[len(refs) - 1 - n_copy : -1]
    buf_ref, out_ref = refs[-2 - n_copy], refs[-3 - n_copy]
    if last:
        buf_ref, out_ref = refs[-2], refs[-3]
    y = place[ZS]

    def copies(buf, blocks, base):
        rows = buf.shape[0] // len(blocks)
        return [
            pltpu.make_async_copy(
                buf.at[pl.ds(v * rows, rows)],
                out_ref.at[place[step], 1 - y if side else y, pl.ds(first_row, rows)],
                sems.at[base + v],
            )
            for v, (step, first_row, side) in enumerate(blocks)
        ]

    going = copies(prev_ref, moved, 0) if moved else []
    for copy in going:
        copy.start()
    for next_ref, copy_ref in zip(next_refs, copy_refs):
        copy_ref[...] = next_ref[...]
    rows = jnp.concatenate([h[...] for h in h_refs], axis=0)
    buf_ref[...] = jnp.dot(rows, vir_ref[...], preferred_element_type=jnp.float32).astype(jnp.bfloat16)
    if last:
        final = copies(buf_ref, made, 4)
        for copy in final:
            copy.start()
        going += final
    for copy in going:
        copy.wait()


def work(state, place, vir, made, hs, out_type, sent=(), after=(), last=False):
    out, buf, moved = state
    rows, nv = hs[0].shape[0], vir.shape[1]
    inside = [vir, *sent, *hs[::-1]] + ([buf] if moved else [])
    ops = [place, *map(vmem, inside), *after] + ([] if out is None else [out])
    block = pltpu.VMEM((len(hs) * rows, nv), jnp.bfloat16)
    results = [] if last else [block] + [pltpu.VMEM(value.shape, value.dtype) for value in sent]
    got = pl.pallas_call(
        functools.partial(work_kernel, moved, made, len(sent), len(after), last),
        in_specs=[IN_SMEM] + [IN_VMEM] * len(inside) + [IN_ANY] * (len(after) + (out is not None)),
        out_specs=[IN_ANY] + [IN_VMEM] * len(results),
        scratch_shapes=([block] if last else []) + [pltpu.SemaphoreType.DMA((8,))],
        out_shape=[out_type] + results,
        input_output_aliases={} if out is None else {len(ops) - 1: 0},
        compiler_params=params(),
        cost_estimate=pl.CostEstimate(flops=PROJ_FLOPS, bytes_accessed=PROJ_BYTES, transcendentals=0),
        name="project",
    )(*ops)
    return (got[0], None if last else got[1], made), *got[2:]


def shards_blocked(integrals, pair_mask, row_blocks, occ_coef, vir_coef):
    mu_dev, fit_dev, nu = integrals.shape
    nocc, nv = occ_coef.shape[1], vir_coef.shape[1]
    share = nocc // 4
    me = lax.axis_index("basis").astype(jnp.int32).reshape(1)
    f = lax.axis_index("fit")
    z, y = f // YS, f % YS
    counts = [fit_dev * part // 16 for part in PARTS]
    starts = [0, counts[0]]

    occ = occ_coef.T
    occs = [occ] + [lax.ppermute(occ, "basis", swap) for swap in (X_SWAP, CORE_SWAP, DIAGONAL)]
    turned, row_blocks, vir, masked = first_order(me, row_blocks, pair_mask, integrals, vir_coef, counts[0])

    held = []
    for k in range(2):
        here, far, send = half_terms(me, row_blocks, occs, turned)
        total, to_x = meet(here, far, lax.ppermute(send, "basis", CORE_SWAP))
        held.append(finish(total, lax.ppermute(to_x, "basis", X_SWAP)))
        if k == 0:
            turned = next_order(masked, starts[1], counts[1], mu_dev)

    place = jnp.concatenate([(z - jnp.arange(ZS)) % ZS, y.reshape(1)]).astype(jnp.int32)
    run = functools.partial(
        work, place=place, vir=vir, out_type=jax.ShapeDtypeStruct((ZS, YS, fit_dev * share, nv), jnp.bfloat16)
    )
    up, down, swap = [functools.partial(lax.ppermute, axis_name="fit", perm=p) for p in (Z_RING, Z_BACK, Y_SWAP)]
    a0, b0 = held
    row_a, row_b = [start * share for start in starts]

    def pair(step, row):
        return [(step, row, 0), (step, row, 1)]

    a1, a0_y = up(a0), swap(a0)
    b1, b0_y = up(b0), swap(b0)
    a2 = up(a1)
    state, a1_copy = run((None, None, None), made=pair(0, row_a), hs=[a0, a0_y], sent=[a1])
    a1_y = swap(a1_copy)
    b2 = up(b1)
    state, b1_copy = run(state, made=pair(0, row_b), hs=[b0, b0_y], sent=[b1])
    b1_y = swap(b1_copy)
    a3 = up(a2)
    state, a2_copy = run(state, made=pair(1, row_a), hs=[a1, a1_y], sent=[a2])
    a2_y = swap(a2_copy)
    b3 = up(b2)
    state, b2_copy, b0_y_copy = run(state, made=pair(1, row_b), hs=[b1, b1_y], sent=[b2, b0_y])
    b2_y = swap(b2_copy)
    b3_y = down(b0_y_copy)
    state, a3_copy = run(state, made=pair(2, row_a), hs=[a2, a2_y], sent=[a3])
    a3_y = swap(a3_copy)
    state, = run(state, made=pair(2, row_b) + [(3, row_a, 0)], hs=[b2, b2_y, a3], after=[b3])
    state, = run(state, made=[(3, row_b, 0)], hs=[b3])
    state, = run(state, made=[(3, row_a, 1), (3, row_b, 1)], hs=[a3_y, b3_y], last=True)
    return state[0].reshape(ZS * YS * fit_dev, share, nv)


def shards(integrals, pair_mask, row_blocks, occ_coef, vir_coef):
    mu_dev = integrals.shape[0]
    fit_dev = integrals.shape[1]
    width_nu = integrals.shape[2]
    nocc = occ_coef.shape[1]
    blocks_dev = mu_dev // BLK
    owned = lax.dynamic_slice_in_dim(row_blocks, lax.axis_index("basis") * blocks_dev, blocks_dev)
    panels = lax.all_gather(occ_coef, "basis", axis=0, tiled=True)
    panel_blocks = panels.reshape(-1, BLK, nocc)
    mask_rows = jnp.take(pair_mask, owned, axis=0).astype(jnp.bfloat16)
    mask_full = jnp.repeat(jnp.repeat(mask_rows, BLK, axis=0), BLK, axis=1)
    masked = integrals * mask_full[:, None, :]
    share = nocc // lax.axis_size("basis")
    occ_rows = jnp.take(panel_blocks, owned, axis=0).reshape(mu_dev, nocc)
    flat = masked.reshape(mu_dev, fit_dev * width_nu)
    summed = lax.psum_scatter(
        lax.dot_general(
            occ_rows, flat, (((0,), (0,)), ((), ())), preferred_element_type=jnp.float32
        ),
        "basis",
        scatter_dimension=0,
        tiled=True,
    )
    half = summed.astype(jnp.bfloat16).reshape(share, fit_dev, width_nu)
    product = jnp.einsum(
        "ipn,na->pia",
        lax.all_gather(half, "fit", axis=1, tiled=True),
        vir_coef,
        preferred_element_type=jnp.float32,
    )
    return product.astype(jnp.bfloat16)


def solution(mesh):
    placed = (P("basis", "fit", None), P(), P(), P("basis", None), P(None, "fit"))
    body = shards_blocked if (mesh.shape["basis"], mesh.shape["fit"]) == (4, ZS * YS) else shards
    return jax.shard_map(body, mesh=mesh, in_specs=placed, out_specs=P(None, "basis", "fit"), check_vma=False)
```
